128 devices in a mesh: section: 8 (over z, y_lo), ctx: 16 (over y_hi, x, core).
Axes of the slice: x: 4, y: 4 (y_hi: 2, y_lo: 2; y = y_hi * 2 + y_lo), z: 4, core: 2. Of those that a mesh axis runs over, the one named last changes fastest.
Arguments:
- query: bfloat16 [8, 6144, 3072], P('section', 'ctx'), may hold values from -200 to 200
- key: bfloat16 [8, 6144, 3072], P('section', 'ctx'), may hold values from -6 to 6
- value: bfloat16 [8, 6144, 3072], P('section', 'ctx'), may hold values from -6 to 6
- out_grad: bfloat16 [8, 6144, 3072], P('section', 'ctx'), may hold values from -6 to 6
- tile_mask: int32 [32, 16], P('ctx'), may hold values from 0 to 1, as said below
Outputs:
- key_grad: bfloat16 [8, 6144, 3072], P('section', 'ctx')
- value_grad: bfloat16 [8, 6144, 3072], P('section', 'ctx')
- upstream: bfloat16 [8, 6144, 3072], P('section', 'ctx')
The draws below stay inside these ranges and needn't reach their ends.
Inputs may be any that keep to these rules, and one draw needn't show every extreme that they name: `tile_mask`: every query tile a reads the key tile a // 2 of its own image rows; the share of ones differs from one pair of query tiles to the next.
All inputs are finite; a program needn't handle non-finite values.
Results may differ from the reference program's by a relative error of at most 0.014.
The reference program's roundings to bfloat16 on the way count: a program that leaves them out, or rounds other values in their place, can miss the bound.
Values may be sent and summed in bfloat16 or wider, within the bound.
No kernel may reach another device: no remote copies, remote signals or barrier semaphores. Data moves between devices by JAX's collectives and lax.ppermute only.
A program may use at most 256 MiB of HBM per device.

```python
import jax
import jax.numpy as jnp
from jax import lax

H = 24
HD = 128
IMG_W = 192
C = 3072
TOK_DEV = 384
POOL_DEV = 96
TOKENS = 6144
SECTIONS = 8
QTILES = 32
KTILES = 16


def draw_query(key, part):
    base = jax.random.normal(jax.random.fold_in(key, 11), (SECTIONS, TOKENS, C), jnp.float32)
    return jnp.clip(base, -200.0, 200.0).astype(jnp.bfloat16)


def draw_tile_mask(key, part):
    qtile = jnp.arange(QTILES, dtype=jnp.int32)
    ktile = jnp.arange(KTILES, dtype=jnp.int32)
    owner = qtile // 2
    level = 1 + owner * 5 % 7
    coins = jax.random.randint(jax.random.fold_in(key, 21), (QTILES, KTILES), 0, 8)
    chosen = coins < level[:, None]
    own = ktile[None, :] == owner[:, None]
    return jnp.where(chosen | own, 1, 0).astype(jnp.int32)


def block_scale(own_key, dims, cuts, smallest, high):
    factor_of, own = 1.0, jax.random.fold_in(own_key, 6)
    for axis_at, blocks in cuts:
        steps = jnp.exp(jax.random.uniform(jax.random.fold_in(own, axis_at), (blocks,), jnp.float32, smallest / len(cuts), high / len(cuts)))
        factor_of = factor_of * jnp.repeat(steps, dims[axis_at] // blocks).reshape([-1 if axis == axis_at else 1 for axis in range(len(dims))])
    return factor_of


def normal_values(rng, dims, deviation, reach, cuts=(), held_as=jnp.bfloat16):
    result = deviation * jax.random.normal(rng, dims, jnp.float32)
    if cuts:
        result = result * block_scale(rng, dims, cuts, -0.22, 0.18)
    return jnp.clip(result, -reach, reach).astype(held_as)


def setup_inputs(seed: int = 0) -> dict:
    arg_keys = jax.random.split(jax.random.key(seed), 6)
    return {
        "query": draw_query(jax.random.fold_in(arg_keys[5], 71), 0),
        "key": normal_values(arg_keys[1], (SECTIONS, TOKENS, C), 1.0, 6.0, ((0, 8), (1, 16))),
        "value": normal_values(arg_keys[2], (SECTIONS, TOKENS, C), 1.0, 6.0, ((0, 8), (1, 16))),
        "out_grad": normal_values(arg_keys[3], (SECTIONS, TOKENS, C), 1.0, 6.0, ((0, 8), (1, 16))),
        "tile_mask": draw_tile_mask(jax.random.fold_in(arg_keys[5], 71), 0),
    }


def pool_rows(data):
    rows = data.shape[0] // IMG_W
    grid = data.astype(jnp.float32).reshape(rows // 2, 2, IMG_W // 2, 2, data.shape[1])
    return grid.mean(axis=(1, 3)).reshape(-1, data.shape[1]).astype(jnp.bfloat16)


def unpool_rows(pooled):
    rows = pooled.shape[0] // (IMG_W // 2)
    grid = (pooled / 4.0).reshape(rows, 1, IMG_W // 2, 1, pooled.shape[1])
    grid = jnp.broadcast_to(grid, (rows, 2, IMG_W // 2, 2, pooled.shape[1]))
    return grid.reshape(-1, pooled.shape[1]).astype(jnp.bfloat16)


def head_backward(qhead, khead, vhead, dhead, allowed):
    scale = 1.0 / (HD ** 0.5)
    scores = jnp.dot(qhead, khead.T, preferred_element_type=jnp.float32) * scale
    scores = jnp.where(allowed, scores, -1e30)
    top = jnp.max(scores, axis=1, keepdims=True)
    expo = jnp.exp(scores - top)
    probs = expo / jnp.sum(expo, axis=1, keepdims=True)
    probs_low = probs.astype(jnp.bfloat16)
    attended = jnp.dot(probs_low, vhead, preferred_element_type=jnp.float32)
    delta = jnp.sum(dhead.astype(jnp.float32) * attended, axis=1, keepdims=True)
    dprob = jnp.dot(dhead, vhead.T, preferred_element_type=jnp.float32)
    score_grad = (probs * (dprob - delta) * scale).astype(jnp.bfloat16)
    qgrad = jnp.dot(score_grad, khead, preferred_element_type=jnp.float32).astype(jnp.bfloat16)
    count = qhead.shape[0] // TOK_DEV
    sg = score_grad.astype(jnp.float32).reshape(count, TOK_DEV, -1)
    pl = probs_low.astype(jnp.float32).reshape(count, TOK_DEV, -1)
    qf = qhead.astype(jnp.float32).reshape(count, TOK_DEV, HD)
    df = dhead.astype(jnp.float32).reshape(count, TOK_DEV, HD)
    kterm = jnp.einsum("ntk,ntd->nkd", sg, qf).astype(jnp.bfloat16).astype(jnp.float32)
    vterm = jnp.einsum("ntk,ntd->nkd", pl, df).astype(jnp.bfloat16).astype(jnp.float32)
    return qgrad, jnp.sum(kterm, axis=0), jnp.sum(vterm, axis=0)


def section_backward(query, key, value, out_grad, allowed):
    pooled_key = pool_rows(key)
    pooled_value = pool_rows(value)
    tokens = query.shape[0]
    def per_head(index):
        start = index * HD
        qh = lax.dynamic_slice_in_dim(query, start, HD, 1)
        kh = lax.dynamic_slice_in_dim(pooled_key, start, HD, 1)
        vh = lax.dynamic_slice_in_dim(pooled_value, start, HD, 1)
        dh = lax.dynamic_slice_in_dim(out_grad, start, HD, 1)
        return head_backward(qh, kh, vh, dh, allowed)
    qgrad, kgrad, vgrad = lax.map(per_head, jnp.arange(H, dtype=jnp.int32))
    qgrad = jnp.transpose(qgrad, (1, 0, 2)).reshape(tokens, H * HD)
    kgrad = jnp.transpose(kgrad, (1, 0, 2)).reshape(-1, H * HD)
    vgrad = jnp.transpose(vgrad, (1, 0, 2)).reshape(-1, H * HD)
    return qgrad, unpool_rows(kgrad), unpool_rows(vgrad)


def reference(query, key, value, out_grad, tile_mask):
    rows_mask = jnp.repeat(tile_mask, IMG_W, axis=0)
    allowed = jnp.repeat(rows_mask, POOL_DEV, axis=1) > 0
    def one_section(items):
        return section_backward(items[0], items[1], items[2], items[3], allowed)
    qgrad, kgrad, vgrad = lax.map(one_section, (query, key, value, out_grad))
    upstream = jnp.concatenate([qgrad[1:], jnp.zeros_like(qgrad[:1])], axis=0)
    return kgrad, vgrad, upstream
```

```python
import functools

import jax
import jax.numpy as jnp
from jax import lax
from jax.experimental import pallas as pl
from jax.experimental.pallas import tpu as pltpu
from jax.sharding import PartitionSpec as P

HD = 128
CHIPS = 8
CORES = 2
HEADS_CHIP = 3
TOK = 384
POOL = 96
ROW = 192
WIDE = HEADS_CHIP * HD
KTILES = CHIPS * CORES
KEYS = KTILES * POOL
SCALE = 1.0 / HD**0.5
LOG2E = 1.4426950408889634
BLOCKED = -1e30
NN = (((1,), (0,)), ((), ()))
NT = (((1,), (1,)), ((), ()))
TN = (((0,), (0,)), ((), ()))


def dot(a, b, dims):
    return lax.dot_general(a, b, dims, preferred_element_type=jnp.float32)


def pool_matrix(shape, token_dim):
    token = lax.broadcasted_iota(jnp.int32, shape, token_dim)
    pooled = lax.broadcasted_iota(jnp.int32, shape, 1 - token_dim)
    column = jnp.where(token >= ROW, token - ROW, token)
    return jnp.where(column // 2 == pooled, 1.0, 0.0).astype(jnp.bfloat16)


def pack_kernel(q_ref, k_ref, v_ref, d_ref, bias_ref, kv_out, qd_out):
    pool = pool_matrix((POOL, TOK), 1)
    kv_out[0, :POOL] = (dot(pool, k_ref[0], NN) * 0.25).astype(jnp.bfloat16)
    kv_out[0, POOL : 2 * POOL] = (dot(pool, v_ref[0], NN) * 0.25).astype(jnp.bfloat16)
    kv_out[0, 2 * POOL :] = bias_ref[...]
    qd_out[0, :TOK] = q_ref[0]
    qd_out[0, TOK:] = d_ref[0]


def pack(query, key, value, out_grad, bias):
    column = pl.BlockSpec((1, TOK, WIDE), lambda j: (0, 0, j))
    return pl.pallas_call(
        pack_kernel,
        grid=(CHIPS,),
        in_specs=[column] * 4 + [pl.BlockSpec((KTILES, TOK), lambda j: (0, 0))],
        out_specs=[
            pl.BlockSpec((1, 2 * POOL + KTILES, WIDE), lambda j: (j, 0, 0)),
            pl.BlockSpec((1, 2 * TOK, WIDE), lambda j: (j, 0, 0)),
        ],
        out_shape=[
            jax.ShapeDtypeStruct((CHIPS, 2 * POOL + KTILES, WIDE), jnp.bfloat16),
            jax.ShapeDtypeStruct((CHIPS, 2 * TOK, WIDE), jnp.bfloat16),
        ],
        name="pack",
    )(query, key, value, out_grad, bias)


def attend_kernel(order_ref, q_ref, d_ref, own_ref, other_ref, bias_ref, *rest):
    dq_refs = rest[:CHIPS]
    dkv_own, dkv_other, keys, values, dkeys, dvalues, expo, dprob = rest[CHIPS:]
    step = pl.program_id(0)

    @pl.when(step == 0)
    def _():
        for s in range(CHIPS):
            for half, ref in enumerate((own_ref, other_ref)):
                at = (half * CHIPS + s) * POOL
                keys[at : at + POOL] = ref[s, :POOL]
                values[at : at + POOL] = ref[s, POOL:]
        dkeys[...] = jnp.zeros_like(dkeys)
        dvalues[...] = jnp.zeros_like(dvalues)

    q = q_ref[0]
    d = d_ref[0]
    part = 4 * POOL
    top = jnp.full((8, TOK), -3e38, jnp.float32)
    for at in range(0, KEYS, part):
        scores = dot(keys[at : at + part], q, NT)
        for tile in range(part // POOL):
            row = at // POOL + tile
            bias = bias_ref[0, row : row + 1].astype(jnp.float32)
            one = scores[tile * POOL : (tile + 1) * POOL] + bias
            expo[at + tile * POOL : at + (tile + 1) * POOL] = one
            top = jnp.maximum(top, jnp.max(one.reshape(POOL // 8, 8, TOK), axis=0))
    top = jnp.max(top, axis=0, keepdims=True)
    total = jnp.zeros((8, TOK), jnp.float32)
    weighted = jnp.zeros((8, TOK), jnp.float32)
    for at in range(0, KEYS, part):
        grad = dot(values[at : at + part], d, NT)
        e = jnp.exp2((expo[at : at + part] - top) * (SCALE * LOG2E))
        expo[at : at + part] = e
        dprob[at : at + part] = grad
        total = total + jnp.sum(e.reshape(part // 8, 8, TOK), axis=0)
        weighted = weighted + jnp.sum((e * grad).reshape(part // 8, 8, TOK), axis=0)
    inverse = 1.0 / jnp.sum(total, axis=0, keepdims=True)
    delta = jnp.sum(weighted, axis=0, keepdims=True) * inverse
    scaled = inverse * SCALE
    dq = jnp.zeros((TOK, HD), jnp.float32)
    for at in range(0, KEYS, part):
        e = expo[at : at + part]
        probs = (e * inverse).astype(jnp.bfloat16)
        sgrad = ((e * scaled) * (dprob[at : at + part] - delta)).astype(jnp.bfloat16)
        dvalues[at : at + part] += dot(probs, d, NN)
        dkeys[at : at + part] += dot(sgrad, q, NN)
        dq = dq + dot(sgrad, keys[at : at + part], TN)
    for k in range(CHIPS):

        @pl.when(step == k)
        def _():
            dq_refs[k][...] = dq.astype(jnp.bfloat16)

    @pl.when(step == CHIPS - 1)
    def _():
        for s in range(CHIPS):
            at = s * POOL
            dkv_own[s, :POOL] = dkeys[at : at + POOL]
            dkv_own[s, POOL:] = dvalues[at : at + POOL]
            at = (CHIPS + s) * POOL
            dkv_other[s, :POOL] = dkeys[at : at + POOL].astype(jnp.bfloat16)
            dkv_other[s, POOL:] = dvalues[at : at + POOL].astype(jnp.bfloat16)


def attend(order, qd, kv_own, kv_other, head):
    whole = lambda k, order: (0, 0, 0)
    return pl.pallas_call(
        attend_kernel,
        grid_spec=pltpu.PrefetchScalarGridSpec(
            num_scalar_prefetch=1,
            grid=(CHIPS,),
            in_specs=[
                pl.BlockSpec((1, TOK, HD), lambda k, order: (order[k], 0, head)),
                pl.BlockSpec((1, TOK, HD), lambda k, order: (order[k], 1, head)),
                pl.BlockSpec((CHIPS, 2 * POOL, HD), lambda k, order: (0, 0, head)),
                pl.BlockSpec((CHIPS, 2 * POOL, HD), lambda k, order: (0, 0, head)),
                pl.BlockSpec((1, KTILES, TOK), lambda k, order: (order[k], 2 * POOL // KTILES, 0)),
            ],
            out_specs=[pl.BlockSpec((TOK, HD), lambda k, order: (0, 0))] * CHIPS
            + [pl.BlockSpec((CHIPS, 2 * POOL, HD), whole)] * 2,
            scratch_shapes=[
                pltpu.VMEM((KEYS, HD), jnp.bfloat16),
                pltpu.VMEM((KEYS, HD), jnp.bfloat16),
                pltpu.VMEM((KEYS, HD), jnp.float32),
                pltpu.VMEM((KEYS, HD), jnp.float32),
                pltpu.VMEM((KEYS, TOK), jnp.float32),
                pltpu.VMEM((KEYS, TOK), jnp.float32),
            ],
        ),
        out_shape=[jax.ShapeDtypeStruct((TOK, HD), jnp.bfloat16)] * CHIPS
        + [
            jax.ShapeDtypeStruct((CHIPS, 2 * POOL, HD), jnp.float32),
            jax.ShapeDtypeStruct((CHIPS, 2 * POOL, HD), jnp.bfloat16),
        ],
        compiler_params=pltpu.CompilerParams(vmem_limit_bytes=40 * 2**20),
        cost_estimate=pl.CostEstimate(
            flops=10 * CHIPS * TOK * KEYS * HD,
            bytes_accessed=6 * 2**20,
            transcendentals=CHIPS * TOK * KEYS,
        ),
        name="attend",
    )(order, qd, qd, kv_own, kv_other, kv_own)


def unpool_kernel(dkv_ref, dk_ref, dv_ref):
    spread = pool_matrix((TOK, POOL), 0)
    dk_ref[0] = (dot(spread, dkv_ref[0, :POOL], NN) * 0.25).astype(jnp.bfloat16)
    dv_ref[0] = (dot(spread, dkv_ref[0, POOL:], NN) * 0.25).astype(jnp.bfloat16)


def unpool(dkv):
    column = pl.BlockSpec((1, TOK, WIDE), lambda j: (0, 0, j))
    whole = jax.ShapeDtypeStruct((1, TOK, CHIPS * WIDE), jnp.bfloat16)
    return pl.pallas_call(
        unpool_kernel,
        grid=(CHIPS,),
        in_specs=[pl.BlockSpec((1, 2 * POOL, WIDE), lambda j: (j, 0, 0))],
        out_specs=[column, column],
        out_shape=[whole, whole],
        name="unpool",
    )(dkv)


def place_kernel(order_ref, *refs):
    pieces, out_ref = refs[:-1], refs[-1]
    step = pl.program_id(0)
    for k in range(CHIPS):

        @pl.when(step == k)
        def _():
            for head in range(HEADS_CHIP):
                out_ref[0, :, head * HD : (head + 1) * HD] = pieces[head * CHIPS + k][...]


def place(order, pieces):
    return pl.pallas_call(
        place_kernel,
        grid_spec=pltpu.PrefetchScalarGridSpec(
            num_scalar_prefetch=1,
            grid=(CHIPS,),
            in_specs=[pl.BlockSpec((TOK, HD), lambda k, order: (0, 0))] * len(pieces),
            out_specs=pl.BlockSpec((1, TOK, WIDE), lambda k, order: (0, 0, order[k])),
        ),
        out_shape=jax.ShapeDtypeStruct((1, TOK, CHIPS * WIDE), jnp.bfloat16),
        compiler_params=pltpu.CompilerParams(vmem_limit_bytes=24 * 2**20),
        name="place",
    )(order, *pieces)


def turned(chip, k, sign):
    outer, inner = k // 4, k % 4
    return (chip // 4 + sign * outer) % 2 * 4 + (chip % 4 + sign * inner) % 4


def shards(query, key, value, out_grad, tile_mask, sections):
    here = lax.axis_index("ctx")
    chip, core = here // CORES, here % CORES
    by_core = tile_mask.reshape(2, CHIPS, CORES)
    own_first = jnp.where(core == 0, by_core, by_core[:, :, ::-1])
    own_first = own_first.transpose(2, 1, 0).reshape(KTILES, 2)
    bias = jnp.where(jnp.repeat(own_first, ROW, axis=1) > 0, 0.0, BLOCKED).astype(jnp.bfloat16)
    kv, qd = pack(query, key, value, out_grad, bias)
    groups = [list(range(c, CHIPS * CORES, CORES)) for c in range(CORES)]
    trade = functools.partial(
        lax.all_to_all, axis_name="ctx", split_axis=0, concat_axis=0, axis_index_groups=groups, tiled=True
    )
    swap = functools.partial(
        lax.ppermute, axis_name="ctx", perm=[(i, i ^ 1) for i in range(CHIPS * CORES)]
    )
    kv_own = trade(kv)
    kv_other = swap(kv_own)
    qd = trade(qd)
    ahead = jnp.stack([turned(chip, k, 1) for k in range(CHIPS)]).astype(jnp.int32)
    behind = jnp.stack([turned(chip, k, -1) for k in range(CHIPS)]).astype(jnp.int32)
    pieces, own_terms, other_terms = [], [], []
    for head in range(HEADS_CHIP):
        *dq, dkv_own, dkv_other = attend(ahead, qd, kv_own, kv_other, head)
        for k in range(CHIPS):
            pairs = [
                (
                    section * KTILES + s * CORES + c,
                    (section - 1) * KTILES + turned(s, k, 1) * CORES + c,
                )
                for section in range(1, sections)
                for s in range(CHIPS)
                for c in range(CORES)
            ]
            pieces.append(lax.ppermute(dq[k], ("section", "ctx"), pairs))
        own_terms.append(dkv_own)
        other_terms.append(swap(dkv_other))
    dkv = [(a + b.astype(jnp.float32)).astype(jnp.bfloat16) for a, b in zip(own_terms, other_terms)]
    dkv = trade(jnp.concatenate(dkv, axis=2))
    key_grad, value_grad = unpool(dkv)
    upstream = place(behind, pieces)
    return key_grad, value_grad, upstream


def solution(mesh):
    spec = P("section", "ctx", None)
    return jax.shard_map(
        functools.partial(shards, sections=mesh.shape["section"]),
        mesh=mesh,
        in_specs=(spec, spec, spec, spec, P("ctx", None)),
        out_specs=(spec, spec, spec),
        check_vma=False,
    )
```

```python
import functools

import jax
import jax.numpy as jnp
from jax import lax
from jax.experimental import pallas as pl
from jax.experimental.pallas import tpu as pltpu
from jax.sharding import PartitionSpec as P

HD = 128
CHIPS = 8
CORES = 2
HEADS_CHIP = 3
TOK = 384
POOL = 96
ROW = 192
WIDE = HEADS_CHIP * HD
KTILES = CHIPS * CORES
KEYS = KTILES * POOL
SCALE = 1.0 / HD**0.5
LOG2E = 1.4426950408889634
BLOCKED = -1e30
LINE = 4
KV_AT = 2 * TOK
BIAS_AT = KV_AT + 2 * POOL
BIAS_ROWS = KTILES * (TOK // HD)
NN = (((1,), (0,)), ((), ()))
NT = (((1,), (1,)), ((), ()))
TN = (((0,), (0,)), ((), ()))


def dot(a, b, dims):
    return lax.dot_general(a, b, dims, preferred_element_type=jnp.float32)


def pool_matrix(shape, token_dim):
    token = lax.broadcasted_iota(jnp.int32, shape, token_dim)
    pooled = lax.broadcasted_iota(jnp.int32, shape, 1 - token_dim)
    column = jnp.where(token >= ROW, token - ROW, token)
    return jnp.where(column // 2 == pooled, 1.0, 0.0).astype(jnp.bfloat16)


def pack_head(pool, out_ref, q, d, k, v):
    out_ref[0, :TOK] = q
    out_ref[0, TOK:KV_AT] = d
    out_ref[0, KV_AT : KV_AT + POOL] = (dot(pool, k, NN) * 0.25).astype(jnp.bfloat16)
    out_ref[0, KV_AT + POOL : BIAS_AT] = (dot(pool, v, NN) * 0.25).astype(jnp.bfloat16)


def pack_first_kernel(core_ref, mask_ref, q_ref, d_ref, k_ref, v_ref, out_ref, pool, bias):
    @pl.when(pl.program_id(0) == 0)
    def _():
        pool[...] = pool_matrix((POOL, TOK), 1)
        for block in range(TOK // HD):
            token = lax.broadcasted_iota(jnp.int32, (1, HD), 1) + block * HD
            for at in range(KTILES):
                tile = at % CHIPS * CORES + (at // CHIPS + core_ref[0]) % CORES
                upper = jnp.where(mask_ref[0, tile] > 0, 0.0, BLOCKED)
                lower = jnp.where(mask_ref[1, tile] > 0, 0.0, BLOCKED)
                row = block * KTILES + at
                bias[row : row + 1] = jnp.where(token < ROW, upper, lower)

    pack_head(pool[...], out_ref, q_ref[0], d_ref[0], k_ref[0], v_ref[0])
    out_ref[0, BIAS_AT:] = bias[...].astype(jnp.bfloat16)


def pack_first(core, tile_mask, arrays):
    rows = BIAS_AT + BIAS_ROWS
    scalars = pl.BlockSpec(memory_space=pltpu.SMEM)
    return pl.pallas_call(
        pack_first_kernel,
        grid=(CHIPS,),
        in_specs=[scalars, scalars] + [pl.BlockSpec((1, TOK, HD), lambda j: (0, 0, HEADS_CHIP * j))] * 4,
        out_specs=pl.BlockSpec((1, rows, HD), lambda j: (j, 0, 0)),
        out_shape=jax.ShapeDtypeStruct((CHIPS, rows, HD), jnp.bfloat16),
        scratch_shapes=[pltpu.VMEM((POOL, TOK), jnp.bfloat16), pltpu.VMEM((BIAS_ROWS, HD), jnp.float32)],
        name="pack_first",
    )(core, tile_mask, *arrays)


def pack_rest_kernel(q_ref, d_ref, k_ref, v_ref, *rest):
    out_refs, pool = rest[:-1], rest[-1]

    @pl.when(pl.program_id(0) == 0)
    def _():
        pool[...] = pool_matrix((POOL, TOK), 1)

    for head, out_ref in enumerate(out_refs, 1):
        columns = slice(head * HD, (head + 1) * HD)
        pack_head(pool[...], out_ref, *[r[0, :, columns] for r in (q_ref, d_ref, k_ref, v_ref)])


def pack_rest(arrays):
    late = HEADS_CHIP - 1
    return pl.pallas_call(
        pack_rest_kernel,
        grid=(CHIPS,),
        in_specs=[pl.BlockSpec((1, TOK, WIDE), lambda j: (0, 0, j))] * 4,
        out_specs=[pl.BlockSpec((1, BIAS_AT, HD), lambda j: (j, 0, 0))] * late,
        out_shape=[jax.ShapeDtypeStruct((CHIPS, BIAS_AT, HD), jnp.bfloat16)] * late,
        scratch_shapes=[pltpu.VMEM((POOL, TOK), jnp.bfloat16)],
        name="pack_rest",
    )(*arrays)


def attend_kernel(order_ref, q_ref, d_ref, own_ref, other_ref, bias_ref, *rest):
    dq_refs, dkv_refs = rest[:-8], rest[-8:-6]
    keys, values, dkeys, dvalues, expo, dprob = rest[-6:]
    step = pl.program_id(0)

    @pl.when(step == 0)
    def _():
        for s in range(CHIPS):
            for half, ref in enumerate((own_ref, other_ref)):
                at = (half * CHIPS + s) * POOL
                keys[at : at + POOL] = ref[s, :POOL]
                values[at : at + POOL] = ref[s, POOL:]
        dkeys[...] = jnp.zeros_like(dkeys)
        dvalues[...] = jnp.zeros_like(dvalues)

    q = q_ref[0]
    d = d_ref[0]
    blocks = [bias_ref[0, at : at + KTILES].astype(jnp.float32) for at in range(0, BIAS_ROWS, KTILES)]
    bias = jnp.concatenate(blocks, axis=1)
    part = 4 * POOL
    top = jnp.full((8, TOK), -3e38, jnp.float32)
    for at in range(0, KEYS, part):
        scores = dot(keys[at : at + part], q, NT)
        for tile in range(part // POOL):
            row = at // POOL + tile
            one = scores[tile * POOL : (tile + 1) * POOL] + bias[row : row + 1]
            expo[at + tile * POOL : at + (tile + 1) * POOL] = one
            top = jnp.maximum(top, jnp.max(one.reshape(POOL // 8, 8, TOK), axis=0))
    top = jnp.max(top, axis=0, keepdims=True)
    total = jnp.zeros((8, TOK), jnp.float32)
    weighted = jnp.zeros((8, TOK), jnp.float32)
    for at in range(0, KEYS, part):
        grad = dot(values[at : at + part], d, NT)
        e = jnp.exp2((expo[at : at + part] - top) * (SCALE * LOG2E))
        expo[at : at + part] = e
        dprob[at : at + part] = grad
        total = total + jnp.sum(e.reshape(part // 8, 8, TOK), axis=0)
        weighted = weighted + jnp.sum((e * grad).reshape(part // 8, 8, TOK), axis=0)
    inverse = 1.0 / jnp.sum(total, axis=0, keepdims=True)
    delta = jnp.sum(weighted, axis=0, keepdims=True) * inverse
    scaled = inverse * SCALE
    dq = jnp.zeros((TOK, HD), jnp.float32)
    for at in range(0, KEYS, part):
        e = expo[at : at + part]
        probs = (e * inverse).astype(jnp.bfloat16)
        sgrad = ((e * scaled) * (dprob[at : at + part] - delta)).astype(jnp.bfloat16)
        dvalues[at : at + part] += dot(probs, d, NN)
        dkeys[at : at + part] += dot(sgrad, q, NN)
        dq = dq + dot(sgrad, keys[at : at + part], TN)
    each = CHIPS // len(dq_refs)
    for k, ref in enumerate(dq_refs):

        @pl.when(step // each == k)
        def _():
            ref[0] = dq.astype(jnp.bfloat16)

    @pl.when(step == CHIPS - 1)
    def _():
        for half, ref in enumerate(dkv_refs):
            for s in range(CHIPS):
                at = (half * CHIPS + s) * POOL
                ref[s, :POOL] = dkeys[at : at + POOL].astype(ref.dtype)
                ref[s, POOL:] = dvalues[at : at + POOL].astype(ref.dtype)


def attend(order, data, first, kv_other, parts):
    each = CHIPS // parts
    terms = pl.BlockSpec((CHIPS, 2 * POOL, HD), lambda k, order: (0, 0, 0))
    return pl.pallas_call(
        attend_kernel,
        grid_spec=pltpu.PrefetchScalarGridSpec(
            num_scalar_prefetch=1,
            grid=(CHIPS,),
            in_specs=[
                pl.BlockSpec((1, TOK, HD), lambda k, order: (order[k], 0, 0)),
                pl.BlockSpec((1, TOK, HD), lambda k, order: (order[k], 1, 0)),
                pl.BlockSpec((CHIPS, 2 * POOL, HD), lambda k, order: (0, KV_AT // (2 * POOL), 0)),
                terms,
                pl.BlockSpec((1, BIAS_ROWS, HD), lambda k, order: (order[k], BIAS_AT // BIAS_ROWS, 0)),
            ],
            out_specs=[
                pl.BlockSpec((1, TOK, HD), lambda k, order, at=at: (jnp.clip(k - at, 0, each - 1), 0, 0))
                for at in range(0, CHIPS, each)
            ]
            + [terms, terms],
            scratch_shapes=[
                pltpu.VMEM((KEYS, HD), jnp.bfloat16),
                pltpu.VMEM((KEYS, HD), jnp.bfloat16),
                pltpu.VMEM((KEYS, HD), jnp.float32),
                pltpu.VMEM((KEYS, HD), jnp.float32),
                pltpu.VMEM((KEYS, TOK), jnp.float32),
                pltpu.VMEM((KEYS, TOK), jnp.float32),
            ],
        ),
        out_shape=[jax.ShapeDtypeStruct((each, TOK, HD), jnp.bfloat16)] * parts
        + [jax.ShapeDtypeStruct((CHIPS, 2 * POOL, HD), t) for t in (jnp.float32, jnp.bfloat16)],
        compiler_params=pltpu.CompilerParams(vmem_limit_bytes=60 * 2**20),
        cost_estimate=pl.CostEstimate(
            flops=40 * CHIPS * TOK * KEYS * HD,
            bytes_accessed=6 * 2**20,
            transcendentals=CHIPS * TOK * KEYS,
        ),
        name="attend",
    )(order, data, data, data, kv_other, first)


def unpool_kernel(*refs):
    dkv_refs, (dk_ref, dv_ref, spread) = refs[:-3], refs[-3:]

    @pl.when(pl.program_id(0) == 0)
    def _():
        spread[...] = pool_matrix((TOK, POOL), 0)

    for head, ref in enumerate(dkv_refs):
        columns = slice(head * HD, (head + 1) * HD)
        part = ref[0] * jnp.bfloat16(0.25)
        dk_ref[0, :, columns] = dot(spread[...], part[:POOL], NN).astype(jnp.bfloat16)
        dv_ref[0, :, columns] = dot(spread[...], part[POOL:], NN).astype(jnp.bfloat16)


def unpool(pieces):
    column = pl.BlockSpec((1, TOK, WIDE), lambda s: (0, 0, s))
    whole = jax.ShapeDtypeStruct((1, TOK, CHIPS * WIDE), jnp.bfloat16)
    return pl.pallas_call(
        unpool_kernel,
        grid=(CHIPS,),
        in_specs=[pl.BlockSpec((1, 2 * POOL, HD), lambda s, at=at // (2 * POOL): (s, at, 0)) for _, at in pieces],
        out_specs=[column, column],
        out_shape=[whole, whole],
        scratch_shapes=[pltpu.VMEM((TOK, POOL), jnp.bfloat16)],
        name="unpool",
    )(*[piece for piece, _ in pieces])


def place_kernel(side_ref, *refs):
    for head, ref in enumerate(refs[:-1]):
        refs[-1][0, :, head * HD : (head + 1) * HD] = ref[0]


def place(side, pieces):
    by_chip = pl.BlockSpec((1, TOK, HD), lambda s, side: (s, 0, 0))
    by_line = pl.BlockSpec((1, TOK, HD), lambda s, side: (s % LINE, (s // LINE + side[0]) % 2, 0))
    return pl.pallas_call(
        place_kernel,
        grid_spec=pltpu.PrefetchScalarGridSpec(
            num_scalar_prefetch=1,
            grid=(CHIPS,),
            in_specs=[by_chip] * (len(pieces) - 1) + [by_line],
            out_specs=pl.BlockSpec((1, TOK, WIDE), lambda s, side: (0, 0, s)),
        ),
        out_shape=jax.ShapeDtypeStruct((1, TOK, CHIPS * WIDE), jnp.bfloat16),
        name="place",
    )(side, *pieces)


def after(value, *others):
    return lax.optimization_barrier((value, *others))[0]


def shards(query, key, value, out_grad, tile_mask, sections):
    here = lax.axis_index("ctx")
    core, side = here % CORES, here // (CORES * LINE)
    members = range(CHIPS * CORES)
    groups = [[i for i in members if i % CORES == c] for c in range(CORES)]

    lines = [group[at : at + LINE] for group in groups for at in (0, LINE)]

    def trade(data, among=groups):
        return lax.all_to_all(data, "ctx", 0, 0, axis_index_groups=among, tiled=True)

    def swap(data):
        return lax.ppermute(data, "ctx", [(i, i ^ 1) for i in members])

    def to_previous(data, across=0):
        pairs = [
            (section * KTILES + i, (section - 1) * KTILES + (i + across * LINE * CORES) % KTILES)
            for section in range(1, sections)
            for i in members
        ]
        return lax.ppermute(data, ("section", "ctx"), pairs)

    def kv_of(data):
        return swap(data[:, KV_AT:BIAS_AT])

    def summed(own, foreign):
        return (own + foreign.astype(jnp.float32)).astype(jnp.bfloat16)

    arrays = (query, out_grad, key, value)
    sent = [pack_first(core.reshape(1), tile_mask, arrays), *pack_rest(arrays)]
    first = after(trade(sent[0]), sent[1])

    natural = jnp.arange(CHIPS, dtype=jnp.int32)
    near_first = (natural // LINE + side) % 2 * LINE + natural % LINE
    dq, own, foreign = attend(natural, first, first, kv_of(first), 1)
    moved, terms = [to_previous(dq)], [(own, swap(foreign))]
    data = after(trade(after(sent[1], first)), dq)
    dq, own, foreign = attend(natural, data, first, kv_of(data), 1)
    moved.append(to_previous(dq))
    terms.append((own, swap(foreign)))
    data = after(trade(after(sent[2], data)), dq)
    joined = jnp.concatenate([moved[0], summed(*terms[0]), summed(*terms[1])], axis=1)
    near, far, own, foreign = attend(near_first, after(data, joined), first, kv_of(data), 2)
    early = after(trade(after(joined, data)), near)
    near, far = to_previous(after(near, moved[1])), to_previous(after(far, moved[1]), 1)
    terms.append((own, swap(foreign)))
    middle = trade(after(jnp.concatenate([moved[1], summed(*terms[2])], axis=1), early))
    late = trade(after(jnp.concatenate([near, far], axis=1), middle), lines)
    key_grad, value_grad = unpool([(early, TOK), (early, TOK + 2 * POOL), (middle, TOK)])
    upstream = place(side.reshape(1), [early, middle, late])
    return key_grad, value_grad, upstream


def solution(mesh):
    spec = P("section", "ctx", None)
    return jax.shard_map(
        functools.partial(shards, sections=mesh.shape["section"]),
        mesh=mesh,
        in_specs=(spec, spec, spec, spec, P("ctx", None)),
        out_specs=(spec, spec, spec),
        check_vma=False,
    )
```

```python
import functools

import jax
import jax.numpy as jnp
from jax import lax
from jax.experimental import pallas as pl
from jax.experimental.pallas import tpu as pltpu
from jax.sharding import PartitionSpec as P

HD = 128
CHIPS = 8
CORES = 2
HEADS_CHIP = 3
TOK = 384
POOL = 96
ROW = 192
WIDE = HEADS_CHIP * HD
KTILES = CHIPS * CORES
KEYS = KTILES * POOL
SCALE = 1.0 / HD**0.5
LOG2E = 1.4426950408889634
BLOCKED = -1e30
LINE = 4
PAIR = 2
WIDTH = PAIR * TOK
KV_AT = 2 * TOK
BIAS_AT = KV_AT + 2 * POOL
BIAS_ROWS = KTILES * (TOK // HD)
NN = (((1,), (0,)), ((), ()))
NT = (((1,), (1,)), ((), ()))
TN = (((0,), (0,)), ((), ()))


def dot(a, b, dims):
    return lax.dot_general(a, b, dims, preferred_element_type=jnp.float32)


def pool_matrix(shape, token_dim):
    token = lax.broadcasted_iota(jnp.int32, shape, token_dim)
    pooled = lax.broadcasted_iota(jnp.int32, shape, 1 - token_dim)
    column = jnp.where(token >= ROW, token - ROW, token)
    return jnp.where(column // 2 == pooled, 1.0, 0.0).astype(jnp.bfloat16)


def pack_head(pool, out_ref, q, d, k, v):
    out_ref[0, :TOK] = q
    out_ref[0, TOK:KV_AT] = d
    out_ref[0, KV_AT : KV_AT + POOL] = (dot(pool, k, NN) * 0.25).astype(jnp.bfloat16)
    out_ref[0, KV_AT + POOL : BIAS_AT] = (dot(pool, v, NN) * 0.25).astype(jnp.bfloat16)


def pack_first_kernel(core_ref, mask_ref, *rest):
    out_ref, pool, bias = rest[-3:]

    @pl.when(pl.program_id(0) == 0)
    def _():
        pool[...] = pool_matrix((POOL, TOK), 1)
        for block in range(TOK // HD):
            token = lax.broadcasted_iota(jnp.int32, (1, HD), 1) + block * HD
            for at in range(KTILES):
                tile = at % CHIPS * CORES + (at // CHIPS + core_ref[0]) % CORES
                upper = jnp.where(mask_ref[0, tile] > 0, 0.0, BLOCKED)
                lower = jnp.where(mask_ref[1, tile] > 0, 0.0, BLOCKED)
                row = block * KTILES + at
                bias[row : row + 1] = jnp.where(token < ROW, upper, lower)

    for chip in range(PAIR):
        pack_head(pool[...], out_ref.at[chip : chip + 1], *[r[0] for r in rest[4 * chip : 4 * chip + 4]])
        out_ref[chip, BIAS_AT:] = bias[...].astype(jnp.bfloat16)


def pack_first(core, tile_mask, arrays):
    rows = BIAS_AT + BIAS_ROWS
    scalars = pl.BlockSpec(memory_space=pltpu.SMEM)
    return pl.pallas_call(
        pack_first_kernel,
        grid=(CHIPS // PAIR,),
        in_specs=[scalars, scalars]
        + [
            pl.BlockSpec((1, TOK, HD), lambda j, chip=chip: (0, 0, HEADS_CHIP * (PAIR * j + chip)))
            for chip in range(PAIR)
            for _ in arrays
        ],
        out_specs=pl.BlockSpec((PAIR, rows, HD), lambda j: (j, 0, 0)),
        out_shape=jax.ShapeDtypeStruct((CHIPS, rows, HD), jnp.bfloat16),
        scratch_shapes=[pltpu.VMEM((POOL, TOK), jnp.bfloat16), pltpu.VMEM((BIAS_ROWS, HD), jnp.float32)],
        name="pack_first",
    )(core, tile_mask, *[*arrays] * PAIR)


def pack_rest_kernel(q_ref, d_ref, k_ref, v_ref, *rest):
    out_refs, pool = rest[:-1], rest[-1]

    @pl.when(pl.program_id(0) == 0)
    def _():
        pool[...] = pool_matrix((POOL, TOK), 1)

    for head, out_ref in enumerate(out_refs, 1):
        columns = slice(head * HD, (head + 1) * HD)
        pack_head(pool[...], out_ref, *[r[0, :, columns] for r in (q_ref, d_ref, k_ref, v_ref)])


def pack_rest(arrays):
    late = HEADS_CHIP - 1
    return pl.pallas_call(
        pack_rest_kernel,
        grid=(CHIPS,),
        in_specs=[pl.BlockSpec((1, TOK, WIDE), lambda j: (0, 0, j))] * 4,
        out_specs=[pl.BlockSpec((1, BIAS_AT, HD), lambda j: (j, 0, 0))] * late,
        out_shape=[jax.ShapeDtypeStruct((CHIPS, BIAS_AT, HD), jnp.bfloat16)] * late,
        scratch_shapes=[pltpu.VMEM((POOL, TOK), jnp.bfloat16)],
        name="pack_rest",
    )(*arrays)


def attend_kernel(side_ref, q_ref, d_ref, own_ref, other_ref, bias_ref, *rest):
    dq_refs, dkv_refs = rest[:-8], rest[-8:-6]
    keys, values, dkeys, dvalues, expo, dprob = rest[-6:]
    step = pl.program_id(0)

    @pl.when(step == 0)
    def _():
        for s in range(CHIPS):
            for half, ref in enumerate((own_ref, other_ref)):
                at = (half * CHIPS + s) * POOL
                keys[at : at + POOL] = ref[s, :POOL]
                values[at : at + POOL] = ref[s, POOL:]
        dkeys[...] = jnp.zeros_like(dkeys)
        dvalues[...] = jnp.zeros_like(dvalues)

    q = q_ref[...].reshape(WIDTH, HD)
    d = d_ref[...].reshape(WIDTH, HD)
    blocks = [
        bias_ref[owner, at : at + KTILES].astype(jnp.float32)
        for owner in range(PAIR)
        for at in range(0, BIAS_ROWS, KTILES)
    ]
    bias = jnp.concatenate(blocks, axis=1)
    part = 4 * POOL
    top = jnp.full((8, WIDTH), -3e38, jnp.float32)
    for at in range(0, KEYS, part):
        scores = dot(keys[at : at + part], q, NT)
        for tile in range(part // POOL):
            row = at // POOL + tile
            one = scores[tile * POOL : (tile + 1) * POOL] + bias[row : row + 1]
            expo[at + tile * POOL : at + (tile + 1) * POOL] = one
            top = jnp.maximum(top, jnp.max(one.reshape(POOL // 8, 8, WIDTH), axis=0))
    top = jnp.max(top, axis=0, keepdims=True)
    total = jnp.zeros((8, WIDTH), jnp.float32)
    weighted = jnp.zeros((8, WIDTH), jnp.float32)
    for at in range(0, KEYS, part):
        grad = dot(values[at : at + part], d, NT)
        e = jnp.exp2((expo[at : at + part] - top) * (SCALE * LOG2E))
        expo[at : at + part] = e
        dprob[at : at + part] = grad
        total = total + jnp.sum(e.reshape(part // 8, 8, WIDTH), axis=0)
        weighted = weighted + jnp.sum((e * grad).reshape(part // 8, 8, WIDTH), axis=0)
    inverse = 1.0 / jnp.sum(total, axis=0, keepdims=True)
    delta = jnp.sum(weighted, axis=0, keepdims=True) * inverse
    scaled = inverse * SCALE
    dq = jnp.zeros((WIDTH, HD), jnp.float32)
    for at in range(0, KEYS, part):
        e = expo[at : at + part]
        probs = (e * inverse).astype(jnp.bfloat16)
        sgrad = ((e * scaled) * (dprob[at : at + part] - delta)).astype(jnp.bfloat16)
        dvalues[at : at + part] += dot(probs, d, NN)
        dkeys[at : at + part] += dot(sgrad, q, NN)
        dq = dq + dot(sgrad, keys[at : at + part], TN)
    each = CHIPS // PAIR // len(dq_refs)
    for k, ref in enumerate(dq_refs):

        @pl.when(step // each == k)
        def _():
            ref[...] = dq.astype(jnp.bfloat16).reshape(PAIR, TOK, HD)

    @pl.when(step == CHIPS // PAIR - 1)
    def _():
        for half, ref in enumerate(dkv_refs):
            for s in range(CHIPS):
                at = (half * CHIPS + s) * POOL
                ref[s, :POOL] = dkeys[at : at + POOL].astype(ref.dtype)
                ref[s, POOL:] = dvalues[at : at + POOL].astype(ref.dtype)


def attend(side, data, first, kv_other, parts):
    each = CHIPS // PAIR // parts
    half = LINE // PAIR

    def owners(k, side):
        return (k // half + side[0]) % 2 * half + k % half

    terms = pl.BlockSpec((CHIPS, 2 * POOL, HD), lambda k, side: (0, 0, 0))
    return pl.pallas_call(
        attend_kernel,
        grid_spec=pltpu.PrefetchScalarGridSpec(
            num_scalar_prefetch=1,
            grid=(CHIPS // PAIR,),
            in_specs=[
                pl.BlockSpec((PAIR, TOK, HD), lambda k, side: (owners(k, side), 0, 0)),
                pl.BlockSpec((PAIR, TOK, HD), lambda k, side: (owners(k, side), 1, 0)),
                pl.BlockSpec((CHIPS, 2 * POOL, HD), lambda k, side: (0, KV_AT // (2 * POOL), 0)),
                terms,
                pl.BlockSpec((PAIR, BIAS_ROWS, HD), lambda k, side: (owners(k, side), BIAS_AT // BIAS_ROWS, 0)),
            ],
            out_specs=[
                pl.BlockSpec((PAIR, TOK, HD), lambda k, side, at=at: (jnp.clip(k - at, 0, each - 1), 0, 0))
                for at in range(0, CHIPS // PAIR, each)
            ]
            + [terms, terms],
            scratch_shapes=[
                pltpu.VMEM((KEYS, HD), jnp.bfloat16),
                pltpu.VMEM((KEYS, HD), jnp.bfloat16),
                pltpu.VMEM((KEYS, HD), jnp.float32),
                pltpu.VMEM((KEYS, HD), jnp.float32),
                pltpu.VMEM((KEYS, WIDTH), jnp.float32),
                pltpu.VMEM((KEYS, WIDTH), jnp.float32),
            ],
        ),
        out_shape=[jax.ShapeDtypeStruct((PAIR * each, TOK, HD), jnp.bfloat16)] * parts
        + [jax.ShapeDtypeStruct((CHIPS, 2 * POOL, HD), t) for t in (jnp.float32, jnp.bfloat16)],
        compiler_params=pltpu.CompilerParams(vmem_limit_bytes=60 * 2**20),
        cost_estimate=pl.CostEstimate(
            flops=40 * CHIPS * TOK * KEYS * HD,
            bytes_accessed=6 * 2**20,
            transcendentals=CHIPS * TOK * KEYS,
        ),
        name="attend",
    )(side, data, data, data, kv_other, first)


def unpool_kernel(*refs):
    dkv_refs, (dk_ref, dv_ref, spread) = refs[:-3], refs[-3:]

    @pl.when(pl.program_id(0) == 0)
    def _():
        spread[...] = pool_matrix((TOK, POOL), 0)

    for chip in range(PAIR):
        for head, ref in enumerate(dkv_refs):
            at = chip * WIDE + head * HD
            part = ref[chip] * jnp.bfloat16(0.25)
            dk_ref[0, :, at : at + HD] = dot(spread[...], part[:POOL], NN).astype(jnp.bfloat16)
            dv_ref[0, :, at : at + HD] = dot(spread[...], part[POOL:], NN).astype(jnp.bfloat16)


def unpool(pieces):
    column = pl.BlockSpec((1, TOK, PAIR * WIDE), lambda s: (0, 0, s))
    whole = jax.ShapeDtypeStruct((1, TOK, CHIPS * WIDE), jnp.bfloat16)
    return pl.pallas_call(
        unpool_kernel,
        grid=(CHIPS // PAIR,),
        in_specs=[
            pl.BlockSpec((PAIR, 2 * POOL, HD), lambda s, at=at // (2 * POOL): (s, at, 0)) for _, at in pieces
        ],
        out_specs=[column, column],
        out_shape=[whole, whole],
        scratch_shapes=[pltpu.VMEM((TOK, POOL), jnp.bfloat16)],
        name="unpool",
    )(*[piece for piece, _ in pieces])


def place_kernel(side_ref, *refs):
    for chip in range(PAIR):
        for head, ref in enumerate(refs[:-1]):
            at = chip * WIDE + head * HD
            refs[-1][0, :, at : at + HD] = ref[chip]


def place(side, by_chip, by_line):
    def line(head):
        per = LINE // PAIR
        return lambda s, side: (s % per, 2 * head + (s // per + side[0]) % 2, 0)

    return pl.pallas_call(
        place_kernel,
        grid_spec=pltpu.PrefetchScalarGridSpec(
            num_scalar_prefetch=1,
            grid=(CHIPS // PAIR,),
            in_specs=[pl.BlockSpec((PAIR, TOK, HD), lambda s, side: (s, 0, 0))]
            + [pl.BlockSpec((PAIR, TOK, HD), line(head)) for head in range(HEADS_CHIP - 1)],
            out_specs=pl.BlockSpec((1, TOK, PAIR * WIDE), lambda s, side: (0, 0, s)),
        ),
        out_shape=jax.ShapeDtypeStruct((1, TOK, CHIPS * WIDE), jnp.bfloat16),
        name="place",
    )(side, by_chip, by_line, by_line)


def after(value, *others):
    return lax.optimization_barrier((value, *others))[0]


def shards(query, key, value, out_grad, tile_mask, sections):
    here = lax.axis_index("ctx")
    core, side = here % CORES, here // (CORES * LINE)
    members = range(CHIPS * CORES)
    groups = [[i for i in members if i % CORES == c] for c in range(CORES)]

    lines = [group[at : at + LINE] for group in groups for at in (0, LINE)]

    def trade(data, among=groups):
        return lax.all_to_all(data, "ctx", 0, 0, axis_index_groups=among, tiled=True)

    def swap(data):
        return lax.ppermute(data, "ctx", [(i, i ^ 1) for i in members])

    def to_previous(data, across=0):
        pairs = [
            (section * KTILES + i, (section - 1) * KTILES + (i + across * LINE * CORES) % KTILES)
            for section in range(1, sections)
            for i in members
        ]
        return lax.ppermute(data, ("section", "ctx"), pairs)

    def kv_of(data):
        return swap(data[:, KV_AT:BIAS_AT])

    def summed(own, foreign):
        return (own + foreign.astype(jnp.float32)).astype(jnp.bfloat16)

    arrays = (query, out_grad, key, value)
    sent = [pack_first(core.reshape(1), tile_mask, arrays), *pack_rest(arrays)]
    first = after(trade(sent[0]), sent[1])

    side = side.reshape(1)
    dq, own, foreign = attend(jnp.zeros((1,), jnp.int32), first, first, kv_of(first), 1)
    moved, terms = [to_previous(dq)], [(own, swap(foreign))]
    data = after(trade(after(sent[1], first)), dq)
    near, far, own, foreign = attend(side, data, first, kv_of(data), 2)
    moved += [to_previous(near), to_previous(far, 1)]
    terms.append((own, swap(foreign)))
    data = after(trade(after(sent[2], data)), near)
    joined = jnp.concatenate([moved[0], summed(*terms[0]), summed(*terms[1])], axis=1)
    near, far, own, foreign = attend(side, after(data, joined), first, kv_of(data), 2)
    early = after(trade(after(joined, data)), near)
    moved += [to_previous(after(near, *moved[1:])), to_previous(after(far, *moved[1:]), 1)]
    middle = trade(after(summed(own, swap(foreign)), early))
    late = trade(after(jnp.concatenate(moved[1:], axis=1), middle), lines)
    key_grad, value_grad = unpool([(early, TOK), (early, TOK + 2 * POOL), (middle, 0)])
    upstream = place(side, early, late)
    return key_grad, value_grad, upstream


def solution(mesh):
    spec = P("section", "ctx", None)
    return jax.shard_map(
        functools.partial(shards, sections=mesh.shape["section"]),
        mesh=mesh,
        in_specs=(spec, spec, spec, spec, P("ctx", None)),
        out_specs=(spec, spec, spec),
        check_vma=False,
    )
```

```python
import functools

import jax
import jax.numpy as jnp
from jax import lax
from jax.experimental import pallas as pl
from jax.experimental.pallas import tpu as pltpu
from jax.sharding import PartitionSpec as P

HD = 128
CHIPS = 8
CORES = 2
HEADS_CHIP = 3
TOK = 384
POOL = 96
ROW = 192
WIDE = HEADS_CHIP * HD
KTILES = CHIPS * CORES
KEYS = KTILES * POOL
SCALE = 1.0 / HD**0.5
LOG2E = 1.4426950408889634
BLOCKED = -1e30
LINE = 4
PAIR = 2
WIDTH = PAIR * TOK
KV_AT = 2 * TOK
BIAS_AT = KV_AT + 2 * POOL
BIAS_ROWS = KTILES
NN = (((1,), (0,)), ((), ()))
NT = (((1,), (1,)), ((), ()))
TN = (((0,), (0,)), ((), ()))


def dot(a, b, dims):
    return lax.dot_general(a, b, dims, preferred_element_type=jnp.float32)


def pool_matrix(shape, token_dim):
    token = lax.broadcasted_iota(jnp.int32, shape, token_dim)
    pooled = lax.broadcasted_iota(jnp.int32, shape, 1 - token_dim)
    column = jnp.where(token >= ROW, token - ROW, token)
    return jnp.where(column // 2 == pooled, 1.0, 0.0).astype(jnp.bfloat16)


def pack_head(pool, out_ref, q, d, k, v):
    out_ref[0, :TOK] = q
    out_ref[0, TOK:KV_AT] = d
    out_ref[0, KV_AT : KV_AT + POOL] = (dot(pool, k, NN) * 0.25).astype(jnp.bfloat16)
    out_ref[0, KV_AT + POOL : BIAS_AT] = (dot(pool, v, NN) * 0.25).astype(jnp.bfloat16)


def pack_first_kernel(core_ref, mask_ref, *rest):
    out_ref, pool, bias = rest[-3:]

    @pl.when(pl.program_id(0) == 0)
    def _():
        pool[...] = pool_matrix((POOL, TOK), 1)
        first = lax.broadcasted_iota(jnp.int32, (1, HD), 1) < HD // 2
        for at in range(KTILES):
            tile = at % CHIPS * CORES + (at // CHIPS + core_ref[0]) % CORES
            upper = jnp.where(mask_ref[0, tile] > 0, 0.0, BLOCKED)
            lower = jnp.where(mask_ref[1, tile] > 0, 0.0, BLOCKED)
            bias[at : at + 1] = jnp.where(first, upper, lower)

    for chip in range(PAIR):
        pack_head(pool[...], out_ref.at[chip : chip + 1], *[r[0] for r in rest[4 * chip : 4 * chip + 4]])
        out_ref[chip, BIAS_AT:] = bias[...].astype(jnp.bfloat16)


def pack_first(core, tile_mask, arrays):
    rows = BIAS_AT + BIAS_ROWS
    scalars = pl.BlockSpec(memory_space=pltpu.SMEM)
    return pl.pallas_call(
        pack_first_kernel,
        grid=(CHIPS // PAIR,),
        in_specs=[scalars, scalars]
        + [
            pl.BlockSpec((1, TOK, HD), lambda j, chip=chip: (0, 0, HEADS_CHIP * (PAIR * j + chip)))
            for chip in range(PAIR)
            for _ in arrays
        ],
        out_specs=pl.BlockSpec((PAIR, rows, HD), lambda j: (j, 0, 0)),
        out_shape=jax.ShapeDtypeStruct((CHIPS, rows, HD), jnp.bfloat16),
        scratch_shapes=[pltpu.VMEM((POOL, TOK), jnp.bfloat16), pltpu.VMEM((BIAS_ROWS, HD), jnp.float32)],
        name="pack_first",
    )(core, tile_mask, *[*arrays] * PAIR)


def pack_rest_kernel(q_ref, d_ref, k_ref, v_ref, *rest):
    out_refs, pool = rest[:-1], rest[-1]

    @pl.when(pl.program_id(0) == 0)
    def _():
        pool[...] = pool_matrix((POOL, TOK), 1)

    for head, out_ref in enumerate(out_refs, 1):
        columns = slice(head * HD, (head + 1) * HD)
        pack_head(pool[...], out_ref, *[r[0, :, columns] for r in (q_ref, d_ref, k_ref, v_ref)])


def pack_rest(arrays):
    late = HEADS_CHIP - 1
    return pl.pallas_call(
        pack_rest_kernel,
        grid=(CHIPS,),
        in_specs=[pl.BlockSpec((1, TOK, WIDE), lambda j: (0, 0, j))] * 4,
        out_specs=[pl.BlockSpec((1, BIAS_AT, HD), lambda j: (j, 0, 0))] * late,
        out_shape=[jax.ShapeDtypeStruct((CHIPS, BIAS_AT, HD), jnp.bfloat16)] * late,
        scratch_shapes=[pltpu.VMEM((POOL, TOK), jnp.bfloat16)],
        name="pack_rest",
    )(*arrays)


def attend_kernel(side_ref, q_ref, d_ref, own_ref, other_ref, bias_ref, *rest):
    dq_refs, dkv_refs = rest[:-8], rest[-8:-6]
    keys, values, dkeys, dvalues, expo, dprob = rest[-6:]
    step = pl.program_id(0)

    @pl.when(step == 0)
    def _():
        for s in range(CHIPS):
            for half, ref in enumerate((own_ref, other_ref)):
                at = (half * CHIPS + s) * POOL
                keys[at : at + POOL] = ref[s, :POOL]
                values[at : at + POOL] = ref[s, POOL:]
        dkeys[...] = jnp.zeros_like(dkeys)
        dvalues[...] = jnp.zeros_like(dvalues)

    q = q_ref[...].reshape(WIDTH, HD)
    d = d_ref[...].reshape(WIDTH, HD)
    upper = lax.broadcasted_iota(jnp.int32, (KTILES, TOK), 1) < ROW
    blocks = []
    for owner in range(PAIR):
        rows = bias_ref[owner].astype(jnp.float32)
        blocks.append(jnp.where(upper, rows[:, :1], rows[:, HD - 1 :]))
    bias = jnp.concatenate(blocks, axis=1)
    part = 4 * POOL
    top = jnp.full((8, WIDTH), -3e38, jnp.float32)
    for at in range(0, KEYS, part):
        scores = dot(keys[at : at + part], q, NT)
        for tile in range(part // POOL):
            row = at // POOL + tile
            one = scores[tile * POOL : (tile + 1) * POOL] + bias[row : row + 1]
            expo[at + tile * POOL : at + (tile + 1) * POOL] = one
            top = jnp.maximum(top, jnp.max(one.reshape(POOL // 8, 8, WIDTH), axis=0))
    top = jnp.max(top, axis=0, keepdims=True)
    total = jnp.zeros((8, WIDTH), jnp.float32)
    weighted = jnp.zeros((8, WIDTH), jnp.float32)
    for at in range(0, KEYS, part):
        grad = dot(values[at : at + part], d, NT)
        e = jnp.exp2((expo[at : at + part] - top) * (SCALE * LOG2E))
        expo[at : at + part] = e
        dprob[at : at + part] = grad
        total = total + jnp.sum(e.reshape(part // 8, 8, WIDTH), axis=0)
        weighted = weighted + jnp.sum((e * grad).reshape(part // 8, 8, WIDTH), axis=0)
    inverse = 1.0 / jnp.sum(total, axis=0, keepdims=True)
    delta = jnp.sum(weighted, axis=0, keepdims=True) * inverse
    scaled = inverse * SCALE
    dq = jnp.zeros((WIDTH, HD), jnp.float32)
    for at in range(0, KEYS, part):
        e = expo[at : at + part]
        probs = (e * inverse).astype(jnp.bfloat16)
        sgrad = ((e * scaled) * (dprob[at : at + part] - delta)).astype(jnp.bfloat16)
        dvalues[at : at + part] += dot(probs, d, NN)
        dkeys[at : at + part] += dot(sgrad, q, NN)
        dq = dq + dot(sgrad, keys[at : at + part], TN)
    each = CHIPS // PAIR // len(dq_refs)
    for k, ref in enumerate(dq_refs):

        @pl.when(step // each == k)
        def _():
            ref[...] = dq.astype(jnp.bfloat16).reshape(PAIR, TOK, HD)

    @pl.when(step == CHIPS // PAIR - 1)
    def _():
        for half, ref in enumerate(dkv_refs):
            for s in range(CHIPS):
                at = (half * CHIPS + s) * POOL
                ref[s, :POOL] = dkeys[at : at + POOL].astype(ref.dtype)
                ref[s, POOL:] = dvalues[at : at + POOL].astype(ref.dtype)


def attend(side, data, first, kv_other, parts):
    each = CHIPS // PAIR // parts
    half = LINE // PAIR

    def owners(k, side):
        return (k // half + side[0]) % 2 * half + k % half

    terms = pl.BlockSpec((CHIPS, 2 * POOL, HD), lambda k, side: (0, 0, 0))
    return pl.pallas_call(
        attend_kernel,
        grid_spec=pltpu.PrefetchScalarGridSpec(
            num_scalar_prefetch=1,
            grid=(CHIPS // PAIR,),
            in_specs=[
                pl.BlockSpec((PAIR, TOK, HD), lambda k, side: (owners(k, side), 0, 0)),
                pl.BlockSpec((PAIR, TOK, HD), lambda k, side: (owners(k, side), 1, 0)),
                pl.BlockSpec((CHIPS, 2 * POOL, HD), lambda k, side: (0, KV_AT // (2 * POOL), 0)),
                terms,
                pl.BlockSpec((PAIR, BIAS_ROWS, HD), lambda k, side: (owners(k, side), BIAS_AT // BIAS_ROWS, 0)),
            ],
            out_specs=[
                pl.BlockSpec((PAIR, TOK, HD), lambda k, side, at=at: (jnp.clip(k - at, 0, each - 1), 0, 0))
                for at in range(0, CHIPS // PAIR, each)
            ]
            + [terms, terms],
            scratch_shapes=[
                pltpu.VMEM((KEYS, HD), jnp.bfloat16),
                pltpu.VMEM((KEYS, HD), jnp.bfloat16),
                pltpu.VMEM((KEYS, HD), jnp.float32),
                pltpu.VMEM((KEYS, HD), jnp.float32),
                pltpu.VMEM((KEYS, WIDTH), jnp.float32),
                pltpu.VMEM((KEYS, WIDTH), jnp.float32),
            ],
        ),
        out_shape=[jax.ShapeDtypeStruct((PAIR * each, TOK, HD), jnp.bfloat16)] * parts
        + [jax.ShapeDtypeStruct((CHIPS, 2 * POOL, HD), t) for t in (jnp.bfloat16, jnp.bfloat16)],
        compiler_params=pltpu.CompilerParams(vmem_limit_bytes=60 * 2**20),
        cost_estimate=pl.CostEstimate(
            flops=40 * CHIPS * TOK * KEYS * HD,
            bytes_accessed=6 * 2**20,
            transcendentals=CHIPS * TOK * KEYS,
        ),
        name="attend",
    )(side, data, data, data, kv_other, first)


def unpool_kernel(*refs):
    dkv_refs, (dk_ref, dv_ref, spread) = refs[:-3], refs[-3:]

    @pl.when(pl.program_id(0) == 0)
    def _():
        spread[...] = pool_matrix((TOK, POOL), 0)

    for chip in range(PAIR):
        for head, ref in enumerate(dkv_refs):
            at = chip * WIDE + head * HD
            part = ref[chip] * jnp.bfloat16(0.25)
            dk_ref[0, :, at : at + HD] = dot(spread[...], part[:POOL], NN).astype(jnp.bfloat16)
            dv_ref[0, :, at : at + HD] = dot(spread[...], part[POOL:], NN).astype(jnp.bfloat16)


def unpool(pieces):
    column = pl.BlockSpec((1, TOK, PAIR * WIDE), lambda s: (0, 0, s))
    whole = jax.ShapeDtypeStruct((1, TOK, CHIPS * WIDE), jnp.bfloat16)
    return pl.pallas_call(
        unpool_kernel,
        grid=(CHIPS // PAIR,),
        in_specs=[
            pl.BlockSpec((PAIR, 2 * POOL, HD), lambda s, at=at // (2 * POOL): (s, at, 0)) for _, at in pieces
        ],
        out_specs=[column, column],
        out_shape=[whole, whole],
        scratch_shapes=[pltpu.VMEM((TOK, POOL), jnp.bfloat16)],
        compiler_params=pltpu.CompilerParams(vmem_limit_bytes=60 * 2**20),
        name="unpool",
    )(*[piece for piece, _ in pieces])


def place_kernel(side_ref, *refs):
    for chip in range(PAIR):
        for head, ref in enumerate(refs[:-1]):
            at = chip * WIDE + head * HD
            refs[-1][0, :, at : at + HD] = ref[chip]


def place(side, by_chip, by_line):
    def line(head):
        per = LINE // PAIR
        return lambda s, side: (s % per, 2 * head + (s // per + side[0]) % 2, 0)

    return pl.pallas_call(
        place_kernel,
        grid_spec=pltpu.PrefetchScalarGridSpec(
            num_scalar_prefetch=1,
            grid=(CHIPS // PAIR,),
            in_specs=[pl.BlockSpec((PAIR, TOK, HD), lambda s, side: (s, 0, 0))]
            + [pl.BlockSpec((PAIR, TOK, HD), line(head)) for head in range(HEADS_CHIP - 1)],
            out_specs=pl.BlockSpec((1, TOK, PAIR * WIDE), lambda s, side: (0, 0, s)),
        ),
        out_shape=jax.ShapeDtypeStruct((1, TOK, CHIPS * WIDE), jnp.bfloat16),
        compiler_params=pltpu.CompilerParams(vmem_limit_bytes=60 * 2**20),
        name="place",
    )(side, by_chip, by_line, by_line)


def after(value, *others):
    return lax.optimization_barrier((value, *others))[0]


def shards(query, key, value, out_grad, tile_mask, sections):
    here = lax.axis_index("ctx")
    core, side = here % CORES, here // (CORES * LINE)
    members = range(CHIPS * CORES)
    groups = [[i for i in members if i % CORES == c] for c in range(CORES)]

    lines = [group[at : at + LINE] for group in groups for at in (0, LINE)]

    def trade(data, among=groups):
        return lax.all_to_all(data, "ctx", 0, 0, axis_index_groups=among, tiled=True)

    def swap(data):
        return lax.ppermute(data, "ctx", [(i, i ^ 1) for i in members])

    def to_previous(data, across=0):
        pairs = [
            (section * KTILES + i, (section - 1) * KTILES + (i + across * LINE * CORES) % KTILES)
            for section in range(1, sections)
            for i in members
        ]
        return lax.ppermute(data, ("section", "ctx"), pairs)

    def kv_of(data):
        return swap(data[:, KV_AT:BIAS_AT])

    def summed(own, foreign):
        return (own.astype(jnp.float32) + foreign.astype(jnp.float32)).astype(jnp.bfloat16)

    arrays = (query, out_grad, key, value)
    sent = [pack_first(core.reshape(1), tile_mask, arrays), *pack_rest(arrays)]
    first = after(trade(sent[0]), sent[1])

    side = side.reshape(1)
    dq, own, foreign = attend(jnp.zeros((1,), jnp.int32), first, first, kv_of(first), 1)
    moved, terms = [to_previous(dq)], [(own, swap(foreign))]
    data = after(trade(after(sent[1], first)), dq)
    near, far, own, foreign = attend(side, data, first, kv_of(data), 2)
    moved += [to_previous(near), to_previous(far, 1)]
    terms.append((own, swap(foreign)))
    data = after(trade(after(sent[2], data)), near)
    joined = jnp.concatenate([moved[0], summed(*terms[0]), summed(*terms[1])], axis=1)
    near, far, own, foreign = attend(side, after(data, joined), first, kv_of(data), 2)
    early = after(trade(after(joined, data)), near)
    moved += [to_previous(after(near, *moved[1:])), to_previous(after(far, *moved[1:]), 1)]
    middle = trade(after(summed(own, swap(foreign)), early))
    late = trade(after(jnp.concatenate(moved[1:], axis=1), middle), lines)
    key_grad, value_grad = unpool([(early, TOK), (early, TOK + 2 * POOL), (middle, 0)])
    upstream = place(side, early, late)
    return key_grad, value_grad, upstream


def solution(mesh):
    spec = P("section", "ctx", None)
    return jax.shard_map(
        functools.partial(shards, sections=mesh.shape["section"]),
        mesh=mesh,
        in_specs=(spec, spec, spec, spec, P("ctx", None)),
        out_specs=(spec, spec, spec),
        check_vma=False,
    )
```

```python
import functools

import jax
import jax.numpy as jnp
from jax import lax
from jax.experimental import pallas as pl
from jax.experimental.pallas import tpu as pltpu
from jax.sharding import PartitionSpec as P

HD = 128
CHIPS = 8
CORES = 2
HEADS_CHIP = 3
TOK = 384
POOL = 96
ROW = 192
WIDE = HEADS_CHIP * HD
KTILES = CHIPS * CORES
KEYS = KTILES * POOL
SCALE = 1.0 / HD**0.5
LOG2E = 1.4426950408889634
BLOCKED = -1e30
LINE = 4
PAIR = 2
WIDTH = PAIR * TOK
KV_AT = 2 * TOK
BIAS_AT = KV_AT + 2 * POOL
BIAS_ROWS = KTILES
NN = (((1,), (0,)), ((), ()))
NT = (((1,), (1,)), ((), ()))
TN = (((0,), (0,)), ((), ()))


def dot(a, b, dims):
    return lax.dot_general(a, b, dims, preferred_element_type=jnp.float32)


def pool_matrix(shape, token_dim):
    token = lax.broadcasted_iota(jnp.int32, shape, token_dim)
    pooled = lax.broadcasted_iota(jnp.int32, shape, 1 - token_dim)
    column = jnp.where(token >= ROW, token - ROW, token)
    return jnp.where(column // 2 == pooled, 1.0, 0.0).astype(jnp.bfloat16)


def pack_head(pool, out_ref, q, d, k, v):
    out_ref[0, :TOK] = q
    out_ref[0, TOK:KV_AT] = d
    out_ref[0, KV_AT : KV_AT + POOL] = (dot(pool, k, NN) * 0.25).astype(jnp.bfloat16)
    out_ref[0, KV_AT + POOL : BIAS_AT] = (dot(pool, v, NN) * 0.25).astype(jnp.bfloat16)


def pack_first_kernel(core_ref, mask_ref, *rest):
    out_ref, pool, bias = rest[-3:]

    @pl.when(pl.program_id(0) == 0)
    def _():
        pool[...] = pool_matrix((POOL, TOK), 1)
        first = lax.broadcasted_iota(jnp.int32, (1, HD), 1) < HD // 2
        for at in range(KTILES):
            tile = at % CHIPS * CORES + (at // CHIPS + core_ref[0]) % CORES
            upper = jnp.where(mask_ref[0, tile] > 0, 0.0, BLOCKED)
            lower = jnp.where(mask_ref[1, tile] > 0, 0.0, BLOCKED)
            bias[at : at + 1] = jnp.where(first, upper, lower)

    for chip in range(PAIR):
        pack_head(pool[...], out_ref.at[chip : chip + 1], *[r[0] for r in rest[4 * chip : 4 * chip + 4]])
        out_ref[chip, BIAS_AT:] = bias[...].astype(jnp.bfloat16)


def pack_first(core, tile_mask, arrays):
    rows = BIAS_AT + BIAS_ROWS
    scalars = pl.BlockSpec(memory_space=pltpu.SMEM)
    return pl.pallas_call(
        pack_first_kernel,
        grid=(CHIPS // PAIR,),
        in_specs=[scalars, scalars]
        + [
            pl.BlockSpec((1, TOK, HD), lambda j, chip=chip: (0, 0, HEADS_CHIP * (PAIR * j + chip)))
            for chip in range(PAIR)
            for _ in arrays
        ],
        out_specs=pl.BlockSpec((PAIR, rows, HD), lambda j: (j, 0, 0)),
        out_shape=jax.ShapeDtypeStruct((CHIPS, rows, HD), jnp.bfloat16),
        scratch_shapes=[pltpu.VMEM((POOL, TOK), jnp.bfloat16), pltpu.VMEM((BIAS_ROWS, HD), jnp.float32)],
        name="pack_first",
    )(core, tile_mask, *[*arrays] * PAIR)


def pack_rest_kernel(q_ref, d_ref, k_ref, v_ref, *rest):
    out_refs, pool = rest[:-1], rest[-1]

    @pl.when(pl.program_id(0) == 0)
    def _():
        pool[...] = pool_matrix((POOL, TOK), 1)

    for head, out_ref in enumerate(out_refs, 1):
        columns = slice(head * HD, (head + 1) * HD)
        pack_head(pool[...], out_ref, *[r[0, :, columns] for r in (q_ref, d_ref, k_ref, v_ref)])


def pack_rest(arrays):
    late = HEADS_CHIP - 1
    return pl.pallas_call(
        pack_rest_kernel,
        grid=(CHIPS,),
        in_specs=[pl.BlockSpec((1, TOK, WIDE), lambda j: (0, 0, j))] * 4,
        out_specs=[pl.BlockSpec((1, BIAS_AT, HD), lambda j: (j, 0, 0))] * late,
        out_shape=[jax.ShapeDtypeStruct((CHIPS, BIAS_AT, HD), jnp.bfloat16)] * late,
        scratch_shapes=[pltpu.VMEM((POOL, TOK), jnp.bfloat16)],
        name="pack_rest",
    )(*arrays)


def attend_kernel(side_ref, q_ref, d_ref, own_ref, other_ref, bias_ref, *rest):
    dq_refs, dkv_refs = rest[:-8], rest[-8:-6]
    keys, values, dkeys, dvalues, expo, dprob = rest[-6:]
    step = pl.program_id(0)

    @pl.when(step == 0)
    def _():
        for s in range(CHIPS):
            for half, ref in enumerate((own_ref, other_ref)):
                at = (half * CHIPS + s) * POOL
                keys[at : at + POOL] = ref[s, :POOL]
                values[at : at + POOL] = ref[s, POOL:]
        dkeys[...] = jnp.zeros_like(dkeys)
        dvalues[...] = jnp.zeros_like(dvalues)

    q = q_ref[...].reshape(WIDTH, HD)
    d = d_ref[...].reshape(WIDTH, HD)
    upper = lax.broadcasted_iota(jnp.int32, (KTILES, TOK), 1) < ROW
    blocks = []
    for owner in range(PAIR):
        rows = bias_ref[owner].astype(jnp.float32)
        blocks.append(jnp.where(upper, rows[:, :1], rows[:, HD - 1 :]))
    bias = jnp.concatenate(blocks, axis=1)
    part = 4 * POOL
    top = jnp.full((8, WIDTH), -3e38, jnp.float32)
    for at in range(0, KEYS, part):
        scores = dot(keys[at : at + part], q, NT)
        for tile in range(part // POOL):
            row = at // POOL + tile
            one = scores[tile * POOL : (tile + 1) * POOL] + bias[row : row + 1]
            expo[at + tile * POOL : at + (tile + 1) * POOL] = one
            top = jnp.maximum(top, jnp.max(one.reshape(POOL // 8, 8, WIDTH), axis=0))
    top = jnp.max(top, axis=0, keepdims=True)
    total = jnp.zeros((8, WIDTH), jnp.float32)
    weighted = jnp.zeros((8, WIDTH), jnp.float32)
    for at in range(0, KEYS, part):
        grad = dot(values[at : at + part], d, NT)
        e = jnp.exp2((expo[at : at + part] - top) * (SCALE * LOG2E))
        expo[at : at + part] = e
        dprob[at : at + part] = grad
        total = total + jnp.sum(e.reshape(part // 8, 8, WIDTH), axis=0)
        weighted = weighted + jnp.sum((e * grad).reshape(part // 8, 8, WIDTH), axis=0)
    inverse = 1.0 / jnp.sum(total, axis=0, keepdims=True)
    delta = jnp.sum(weighted, axis=0, keepdims=True) * inverse
    scaled = inverse * SCALE
    dq = jnp.zeros((WIDTH, HD), jnp.float32)
    for at in range(0, KEYS, part):
        e = expo[at : at + part]
        probs = (e * inverse).astype(jnp.bfloat16)
        sgrad = ((e * scaled) * (dprob[at : at + part] - delta)).astype(jnp.bfloat16)
        dvalues[at : at + part] += dot(probs, d, NN)
        dkeys[at : at + part] += dot(sgrad, q, NN)
        dq = dq + dot(sgrad, keys[at : at + part], TN)
    each = CHIPS // PAIR // len(dq_refs)
    for k, ref in enumerate(dq_refs):

        @pl.when(step // each == k)
        def _():
            ref[...] = dq.astype(jnp.bfloat16).reshape(PAIR, TOK, HD)

    @pl.when(step == CHIPS // PAIR - 1)
    def _():
        for half, ref in enumerate(dkv_refs):
            for s in range(CHIPS):
                at = (half * CHIPS + s) * POOL
                ref[s, :POOL] = dkeys[at : at + POOL].astype(ref.dtype)
                ref[s, POOL:] = dvalues[at : at + POOL].astype(ref.dtype)


def attend(side, data, first, kv_other, parts):
    each = CHIPS // PAIR // parts
    half = LINE // PAIR

    def owners(k, side):
        return (k // half + side[0]) % 2 * half + k % half

    terms = pl.BlockSpec((CHIPS, 2 * POOL, HD), lambda k, side: (0, 0, 0))
    return pl.pallas_call(
        attend_kernel,
        grid_spec=pltpu.PrefetchScalarGridSpec(
            num_scalar_prefetch=1,
            grid=(CHIPS // PAIR,),
            in_specs=[
                pl.BlockSpec((PAIR, TOK, HD), lambda k, side: (owners(k, side), 0, 0)),
                pl.BlockSpec((PAIR, TOK, HD), lambda k, side: (owners(k, side), 1, 0)),
                pl.BlockSpec((CHIPS, 2 * POOL, HD), lambda k, side: (0, KV_AT // (2 * POOL), 0)),
                terms,
                pl.BlockSpec((PAIR, BIAS_ROWS, HD), lambda k, side: (owners(k, side), BIAS_AT // BIAS_ROWS, 0)),
            ],
            out_specs=[
                pl.BlockSpec((PAIR, TOK, HD), lambda k, side, at=at: (jnp.clip(k - at, 0, each - 1), 0, 0))
                for at in range(0, CHIPS // PAIR, each)
            ]
            + [terms, terms],
            scratch_shapes=[
                pltpu.VMEM((KEYS, HD), jnp.bfloat16),
                pltpu.VMEM((KEYS, HD), jnp.bfloat16),
                pltpu.VMEM((KEYS, HD), jnp.float32),
                pltpu.VMEM((KEYS, HD), jnp.float32),
                pltpu.VMEM((KEYS, WIDTH), jnp.float32),
                pltpu.VMEM((KEYS, WIDTH), jnp.float32),
            ],
        ),
        out_shape=[jax.ShapeDtypeStruct((PAIR * each, TOK, HD), jnp.bfloat16)] * parts
        + [jax.ShapeDtypeStruct((CHIPS, 2 * POOL, HD), t) for t in (jnp.bfloat16, jnp.bfloat16)],
        compiler_params=pltpu.CompilerParams(vmem_limit_bytes=60 * 2**20),
        cost_estimate=pl.CostEstimate(
            flops=40 * CHIPS * TOK * KEYS * HD,
            bytes_accessed=6 * 2**20,
            transcendentals=CHIPS * TOK * KEYS,
        ),
        name="attend",
    )(side, data, data, data, kv_other, first)


def unpool_kernel(*refs):
    dkv_refs, (dk_ref, dv_ref, spread) = refs[:-3], refs[-3:]

    @pl.when(pl.program_id(0) == 0)
    def _():
        spread[...] = pool_matrix((TOK, POOL), 0)

    for chip in range(PAIR):
        for head, ref in enumerate(dkv_refs):
            at = chip * WIDE + head * HD
            part = ref[chip] * jnp.bfloat16(0.25)
            dk_ref[0, :, at : at + HD] = dot(spread[...], part[:POOL], NN).astype(jnp.bfloat16)
            dv_ref[0, :, at : at + HD] = dot(spread[...], part[POOL:], NN).astype(jnp.bfloat16)


def unpool(pieces):
    column = pl.BlockSpec((1, TOK, PAIR * WIDE), lambda s: (0, 0, s))
    whole = jax.ShapeDtypeStruct((1, TOK, CHIPS * WIDE), jnp.bfloat16)
    return pl.pallas_call(
        unpool_kernel,
        grid=(CHIPS // PAIR,),
        in_specs=[
            pl.BlockSpec((PAIR, 2 * POOL, HD), lambda s, at=at // (2 * POOL): (s, at, 0)) for _, at in pieces
        ],
        out_specs=[column, column],
        out_shape=[whole, whole],
        scratch_shapes=[pltpu.VMEM((TOK, POOL), jnp.bfloat16)],
        compiler_params=pltpu.CompilerParams(vmem_limit_bytes=60 * 2**20),
        name="unpool",
    )(*[piece for piece, _ in pieces])


def place_kernel(side_ref, *refs):
    for chip in range(PAIR):
        for head, ref in enumerate(refs[:-1]):
            at = chip * WIDE + head * HD
            refs[-1][0, :, at : at + HD] = ref[chip]


def place(side, by_chip, by_line):
    def line(head):
        per = LINE // PAIR
        return lambda s, side: (s % per, 2 * head + (s // per + side[0]) % 2, 0)

    return pl.pallas_call(
        place_kernel,
        grid_spec=pltpu.PrefetchScalarGridSpec(
            num_scalar_prefetch=1,
            grid=(CHIPS // PAIR,),
            in_specs=[pl.BlockSpec((PAIR, TOK, HD), lambda s, side: (s, 0, 0))]
            + [pl.BlockSpec((PAIR, TOK, HD), line(head)) for head in range(HEADS_CHIP - 1)],
            out_specs=pl.BlockSpec((1, TOK, PAIR * WIDE), lambda s, side: (0, 0, s)),
        ),
        out_shape=jax.ShapeDtypeStruct((1, TOK, CHIPS * WIDE), jnp.bfloat16),
        compiler_params=pltpu.CompilerParams(vmem_limit_bytes=60 * 2**20),
        name="place",
    )(side, by_chip, by_line, by_line)


def after(value, *others):
    return lax.optimization_barrier((value, *others))[0]


def shards(query, key, value, out_grad, tile_mask, sections):
    here = lax.axis_index("ctx")
    core, side = here % CORES, here // (CORES * LINE)
    members = range(CHIPS * CORES)
    groups = [[i for i in members if i % CORES == c] for c in range(CORES)]

    lines = [group[at : at + LINE] for group in groups for at in (0, LINE)]

    def trade(data, among=groups):
        return lax.all_to_all(data, "ctx", 0, 0, axis_index_groups=among, tiled=True)

    def swap(data):
        return lax.ppermute(data, "ctx", [(i, i ^ 1) for i in members])

    def to_previous(data, across=0):
        pairs = [
            (section * KTILES + i, (section - 1) * KTILES + (i + across * LINE * CORES) % KTILES)
            for section in range(1, sections)
            for i in members
        ]
        return lax.ppermute(data, ("section", "ctx"), pairs)

    def kv_of(data):
        return swap(data[:, KV_AT:BIAS_AT])

    def summed(own, foreign):
        return (own.astype(jnp.float32) + foreign.astype(jnp.float32)).astype(jnp.bfloat16)

    arrays = (query, out_grad, key, value)
    sent = [pack_first(core.reshape(1), tile_mask, arrays), *pack_rest(arrays)]
    first = after(trade(sent[0]), sent[1])

    side = side.reshape(1)
    dq, own, foreign = attend(jnp.zeros((1,), jnp.int32), first, first, kv_of(first), 1)
    terms = [(own, swap(foreign))]
    data = after(trade(after(sent[1], first)), dq)
    other = kv_of(data)
    moved = [to_previous(after(dq, other))]
    near, far, own, foreign = attend(side, data, first, other, 2)
    moved += [to_previous(near), to_previous(far, 1)]
    terms.append((own, swap(foreign)))
    data = after(trade(after(sent[2], data)), near)
    joined = jnp.concatenate([summed(*terms[0]), summed(*terms[1])], axis=1)
    near, far, own, foreign = attend(side, after(data, joined), first, kv_of(data), 2)
    foreign = after(foreign, *moved)
    early = after(trade(after(joined, data)), near)
    moved += [to_previous(after(near, *moved)), to_previous(after(far, *moved), 1)]
    middle = trade(after(jnp.concatenate([moved[0], summed(own, swap(foreign))], axis=1), early))
    late = trade(after(jnp.concatenate(moved[1:], axis=1), middle), lines)
    key_grad, value_grad = unpool([(early, 0), (early, 2 * POOL), (middle, TOK)])
    upstream = place(side, middle, late)
    return key_grad, value_grad, upstream


def solution(mesh):
    spec = P("section", "ctx", None)
    return jax.shard_map(
        functools.partial(shards, sections=mesh.shape["section"]),
        mesh=mesh,
        in_specs=(spec, spec, spec, spec, P("ctx", None)),
        out_specs=(spec, spec, spec),
        check_vma=False,
    )
```
